768 devices in a mesh: section: 16 (over y_hi, x, core), shard: 12 (over z), replica: 4 (over y_lo).
Axes of the slice: x: 4, y: 8 (y_hi: 2, y_lo: 4; y = y_hi * 4 + y_lo), z: 12, core: 2. Of those that a mesh axis runs over, the one named last changes fastest.
Arguments:
- normed: bfloat16 [16, 2, 6144, 4096], P('section', None, ('shard', 'replica')), may hold values from -0.0546875 to 0.0546875
- key_cotangent: bfloat16 [16, 2, 6144, 512], P('section', None, ('shard', 'replica')), may hold values from -12 to 12
- positions: int32 [2, 6144], P(None, ('shard', 'replica')), may hold values from 0 to 1023, as said below
- key_weight: bfloat16 [16, 4128, 512], P('section', 'shard'), may hold values from -0.09375 to 0.09375
Outputs:
- key_weight_grad: bfloat16 [16, 4128, 512], P('section', 'shard')
- passed_grad: bfloat16 [16, 2, 6144, 4096], P('section', None, ('shard', 'replica'))
The draws below stay inside these ranges and needn't reach their ends.
Inputs may be any that keep to these rules, and one draw needn't show every extreme that they name: `positions`: each token's position within its document of the micro-batch; in every micro-batch a document begins at every multiple of 1024 tokens, and in all but the first micro-batch at further places drawn at random.
All inputs are finite; a program needn't handle non-finite values.
Results may differ from the reference program's by a relative error of at most 0.018.
Values may be sent and summed in bfloat16 or wider, within the bound.
A program may use at most 64 MiB of HBM per device.

```python
import jax
import jax.numpy as jnp
from jax import lax

DW = 4096
KH = 4
HEAD = 128
MB = 2
KW = 512
DW_PAD = 4128
SECTIONS = 16
TOKENS = 6144
N_SHARD = 12
N_REPLICA = 4


def draw_positions(key, part):
    index = jnp.arange(TOKENS, dtype=jnp.int32)
    first_key = jax.random.fold_in(key, 11)
    extra_key = jax.random.fold_in(key, 23)
    span = min(TOKENS, 1024)
    forced = jax.random.randint(first_key, (MB, 1), 1, span)
    fresh = jax.random.randint(extra_key, (MB, TOKENS), 0, 64) == 0
    later = (jnp.arange(MB, dtype=jnp.int32) > 0)[:, None]
    chosen = jnp.logical_or(fresh, index[None, :] == forced)
    starts = jnp.logical_or(jnp.logical_and(chosen, later), (index % 1024 == 0)[None, :])
    marks = jnp.where(starts, index[None, :], 0)
    return (index[None, :] - lax.cummax(marks, axis=1)).astype(jnp.int32)


def level_of(rng, shape, shards, smallest, largest):
    def one(axis_at, shards_of):
        heights = jax.random.uniform(jax.random.fold_in(jax.random.fold_in(rng, 6), axis_at), (shards_of,), jnp.float32, smallest / len(shards), largest / len(shards))
        return jnp.repeat(jnp.exp(heights), shape[axis_at] // shards_of).reshape((-1,) + (1,) * (len(shape) - axis_at - 1))

    level = one(*shards[0])
    for cut in shards[1:]:
        level = level * one(*cut)
    return level


def bell_draw(rng, extent, deviation, bound, pieces=(), kind=jnp.bfloat16):
    gain = level_of(rng, extent, pieces, -0.22, 0.18) if pieces else 1.0
    values = jax.random.normal(rng, extent, jnp.float32) * deviation * gain
    return jnp.minimum(jnp.maximum(values, -bound), bound).astype(kind)


def setup_inputs(seed: int = 0) -> dict:
    key_list = jax.random.split(jax.random.key(seed), 5)
    return {
        "normed": bell_draw(key_list[0], (SECTIONS, MB, TOKENS, DW), (MB * TOKENS) ** -0.5, 0.0546875, ((0, 16), (2, 48))),
        "key_cotangent": bell_draw(key_list[1], (SECTIONS, MB, TOKENS, KW), 2.0, 12.0, ((0, 16), (2, 48))),
        "positions": draw_positions(jax.random.fold_in(key_list[4], 71), 0),
        "key_weight": bell_draw(key_list[3], (SECTIONS, DW_PAD, KW), DW ** -0.5, 0.09375, ((0, 16), (1, 12))),
    }


def undo_rotation(cotangent, positions):
    half = HEAD // 2
    index = jnp.arange(half, dtype=jnp.float32)
    freq = jnp.power(jnp.float32(500000.0), -2.0 * index / HEAD)
    angle = positions.astype(jnp.float32)[..., None] * freq
    angle = jnp.concatenate([angle, angle], axis=-1)[:, :, None, :]
    cosine = jnp.cos(angle)
    sine = jnp.sin(angle)
    lead = cotangent.shape[:2]
    grads = cotangent.astype(jnp.float32).reshape(lead + (KH, HEAD))
    swapped = jnp.concatenate([grads[..., half:], -grads[..., :half]], axis=-1)
    result = grads * cosine + swapped * sine
    return result.reshape(lead + (KH * HEAD,)).astype(jnp.bfloat16)


def section_work(items, positions):
    normed, cotangent, weight = items
    key_grad = undo_rotation(cotangent, positions)
    input_grad = jnp.einsum("mtk,dk->mtd", key_grad.astype(jnp.float32),
                            weight[:DW].astype(jnp.float32)).astype(jnp.bfloat16)
    per_dev = TOKENS // (N_SHARD * N_REPLICA)
    blocks_in = normed.reshape(MB, N_SHARD, N_REPLICA, per_dev, DW).astype(jnp.float32)
    blocks_key = key_grad.reshape(MB, N_SHARD, N_REPLICA, per_dev, KH * HEAD).astype(jnp.float32)
    terms = jnp.einsum("mcrtd,mcrtk->crdk", blocks_in, blocks_key).astype(jnp.bfloat16)
    terms = lax.optimization_barrier(terms).astype(jnp.float32)
    shard_sum = jnp.sum(terms, axis=0).astype(jnp.bfloat16)
    shard_sum = lax.optimization_barrier(shard_sum).astype(jnp.float32)
    grad = jnp.sum(shard_sum, axis=0).astype(jnp.bfloat16)
    padding = jnp.zeros((weight.shape[0] - DW, KH * HEAD), jnp.bfloat16)
    return input_grad, jnp.concatenate([grad, padding], axis=0)


def reference(normed, key_cotangent, positions, key_weight):
    input_grad, weight_grad = lax.map(lambda items: section_work(items, positions),
                                      (normed, key_cotangent, key_weight))
    passed = jnp.concatenate([input_grad[1:], jnp.zeros_like(input_grad[:1])], axis=0)
    return weight_grad, passed
```

```python
import functools

import jax
import jax.numpy as jnp
import numpy as np
from jax import lax
from jax.experimental import pallas as pl
from jax.experimental.pallas import tpu as pltpu
from jax.sharding import PartitionSpec as P

HEAD = 128
RING = 12
ROWS = 344
PAD = 352
KW = 512
TOK = 256
WIDTH = 4096
LAST = 15
CHUNKS = ((0, 96), (96, 96), (192, 80), (272, 80))
NC = len(CHUNKS)
MESH = pl.DeviceIdType.MESH
SUM_EVEN, SUM_ODD = (6, 4, -4, 2, -2, 0), (5, -5, 3, -3, 1, -1)
GET_EVEN, GET_ODD = (0, -2, 2, -4, 4, -6), (-1, 1, -3, 3, -5, 5)
F32, BF16 = jnp.float32, jnp.bfloat16


def kernel(
    normed_hbm, cot_ref, pos_ref, freq_ref, w_ref,
    grad_ref, out_ref,
    normed, flat, send_n, got_n, key, key_next, wsrc, weights, terms, sums,
    cols, send_c, got_c, part, part_in, total_in,
    local_sem, w_sem, k_sem, n_sem, g_sem, r_sem, c_sem, x_sem, t_sem,
):
    s, z, r = (lax.axis_index(a) for a in ("section", "shard", "replica"))
    parity = lax.rem(r, 2)
    odd = lax.rem(z + parity, 2)
    even = odd == 0
    is_odd = odd == 1
    sign = 1 - 2 * lax.rem(s, 2)
    mate = (s, z, r + 1 - 2 * parity)
    across = (s, z, lax.rem(r + 2, 4))
    ahead = (s, lax.rem(z + sign + RING, RING), r)
    behind = (s, lax.rem(z - sign + RING, RING), r)
    before = (jnp.maximum(s - 1, 0), z, r)
    after = (jnp.minimum(s + 1, LAST), z, r)
    to = (ahead, behind)

    def owner(pair, which):
        step = jnp.where(which == 0, pair[0], pair[1])
        return lax.rem(z + sign * step + 2 * RING, RING)

    pending = []

    def push(src, dst, sems, index, device, when=None):
        copy = pltpu.make_async_remote_copy(
            src, dst, sems.at[(0,) + index[0]], sems.at[(1,) + index[1]],
            device_id=device, device_id_type=MESH,
        )
        if when is None:
            copy.start()
        else:
            pl.when(when)(copy.start)
        pending.append((when, copy))

    def arrived(dst, sems, index):
        pltpu.make_async_remote_copy(
            dst, dst, sems.at[(0,) + index], sems.at[(1,) + index],
            device_id=mate, device_id_type=MESH,
        ).wait_recv()

    fetch = pltpu.make_async_copy(normed_hbm, normed, local_sem)
    fetch.start()
    barrier = pltpu.get_barrier_semaphore()
    for device in (mate, across, ahead, behind):
        pl.semaphore_signal(barrier, inc=1, device_id=device, device_id_type=MESH)

    @pl.when(s > 0)
    def _():
        pl.semaphore_signal(barrier, inc=1, device_id=before, device_id_type=MESH)

    @pl.when(s < LAST)
    def _():
        pl.semaphore_signal(barrier, inc=1, device_id=after, device_id_type=MESH)

    wsrc[...] = jnp.concatenate(
        [w_ref[...].astype(F32), jnp.zeros((PAD - ROWS, KW), F32)], axis=0
    ).astype(BF16)

    half = lax.broadcasted_iota(jnp.int32, (TOK // 2, HEAD), 1) < HEAD // 2
    for m in range(2):
        place = jnp.broadcast_to(pos_ref[m : m + 1, :].astype(F32), (HEAD, HEAD)).T
        angle = place * freq_ref[...]
        cosine = jnp.cos(angle)
        sine = jnp.sin(angle)
        sine = jnp.where(half, sine, -sine)
        rows = pl.ds(m * (TOK // 2), TOK // 2)
        for h in range(KW // HEAD):
            lanes = pl.ds(h * HEAD, HEAD)
            g = cot_ref[rows, lanes].astype(F32)
            key[0, rows, lanes] = (
                g * cosine + pltpu.roll(g, HEAD // 2, 1) * sine
            ).astype(BF16)

    pl.semaphore_wait(
        barrier, 4 + (s > 0).astype(jnp.int32) + (s < LAST).astype(jnp.int32)
    )

    mine = lax.div(z, 2)
    for c, (at, size) in enumerate(CHUNKS):
        rows = pl.ds(at, size)
        push(wsrc.at[rows], weights.at[mine, rows], w_sem, ((c,), (c,)), before,
             jnp.logical_and(s > 0, even))
    push(key.at[0], key.at[1], k_sem, ((0,), (0,)), mate)
    push(key.at[0], key_next.at[0], k_sem, ((1,), (1,)), before, s > 0)

    @pl.when(s == LAST)
    def _():
        key_next[...] = jnp.zeros_like(key_next)

        @pl.when(even)
        def _():
            weights[mine] = wsrc[...]

    fetch.wait()
    for i in range(WIDTH // 512):
        flat[pl.ds(512 * i, 512), :] = normed[:, pl.ds(512 * i, 512)].astype(F32).T
    flat[pl.ds(WIDTH, 40), :] = jnp.zeros((40, TOK), F32)

    def block(o):
        return flat[pl.ds(pl.multiple_of(ROWS * o, 8), PAD), :].astype(BF16)

    for n in range(6):
        send_n[n] = block(owner((SUM_ODD[n], SUM_EVEN[n]), odd))
        push(send_n.at[n], got_n.at[n], n_sem, ((n,), (n,)), mate)

    for c, (at, size) in enumerate(CHUNKS):
        rows = pl.ds(at, size)

        @pl.when(jnp.logical_and(s < LAST, even))
        def _():
            arrived(weights.at[mine, rows], w_sem, (c,))

        for d in range(2):
            push(weights.at[mine, rows], weights.at[mine, rows], g_sem,
                 ((d, 0, c), (d, 0, c)), to[d], even)

    arrived(key.at[1], k_sem, (0,))
    push(key.at[1], key_next.at[1], k_sem, ((2,), (2,)), before, s > 0)

    def term(n):
        arrived(got_n.at[n], n_sem, (n,))
        own = block(owner((SUM_EVEN[n], SUM_ODD[n]), odd))
        terms[n] = (
            jnp.dot(own, key[0], preferred_element_type=F32)
            + jnp.dot(got_n[n], key[1], preferred_element_type=F32)
        ).astype(BF16)

    def gather_step(j):
        for c, (at, size) in enumerate(CHUNKS):
            rows = pl.ds(at, size)
            for d in range(2):
                away = 2 * j + 2 - odd
                from_ = lax.rem(z + (2 * d - 1) * sign * away + 2 * RING, RING)
                spot = weights.at[lax.div(from_, 2), rows]
                if j == 2 and d == 1:
                    pl.when(is_odd)(lambda: arrived(spot, g_sem, (d, j, c)))
                    continue
                arrived(spot, g_sem, (d, j, c))
                slot = j + 1 - odd
                if j < 2:
                    push(spot, spot, g_sem, ((d, slot, c), (d, slot, c)), to[d])
                else:
                    push(spot, spot, g_sem, ((d, 2, c), (d, 2, c)), to[d], is_odd)

    def column(n):
        o = owner((GET_EVEN[n], GET_ODD[n]), odd)
        both = lax.dot_general(
            weights[lax.div(o, 2)], key_next[...].reshape(2 * TOK, KW),
            (((1,), (1,)), ((), ())), preferred_element_type=F32,
        )
        cols[pl.ds(pl.multiple_of(ROWS * o, 8), ROWS), :] = both[:ROWS, :TOK]
        send_c[n] = both[:, TOK:].astype(BF16)
        push(send_c.at[n], got_c.at[n], c_sem, ((n,), (n,)), mate)

    def sum_start():
        for c, (at, size) in enumerate(CHUNKS):
            rows = pl.ds(at, size)
            push(terms.at[0, rows], sums.at[0, 0, rows], r_sem, ((0, 0, c), (0, 0, c)),
                 to[0], even)

    def sum_step(j):
        for c, (at, size) in enumerate(CHUNKS):
            rows = pl.ds(at, size)
            for d in range(2):
                n = 2 * j + d + 1 - odd
                slot = j + 1 - odd
                spot = sums.at[d, j, rows]
                there = sums.at[d, slot, rows]

                def add():
                    arrived(spot, r_sem, (d, j, c))
                    spot[...] = (
                        spot[...].astype(F32) + terms[n, rows].astype(F32)
                    ).astype(BF16)

                if (d, j) == (1, 0):
                    pl.when(even)(add)
                    push(spot, there, r_sem, ((d, 1, c), (d, 1, c)), to[d], even)
                    push(terms.at[n, rows], there, r_sem, ((d, 0, c), (d, 0, c)), to[d],
                         is_odd)
                elif j < 2:
                    add()
                    push(spot, there, r_sem, ((d, slot, c), (d, slot, c)), to[d])
                else:
                    pl.when(is_odd)(add)
                    push(spot, sums.at[d, 2, rows], r_sem, ((d, 2, c), (d, 2, c)), to[d],
                         is_odd)
            if j == 2:

                @pl.when(even)
                def _():
                    for d in range(2):
                        arrived(sums.at[d, 2, rows], r_sem, (d, 2, c))
                    part[rows] = (
                        terms[5, rows].astype(F32)
                        + sums[0, 2, rows].astype(F32)
                        + sums[1, 2, rows].astype(F32)
                    ).astype(BF16)

                push(part.at[rows], part_in.at[rows], x_sem, ((c,), (c,)), across, even)

    gather_step(0)

    @pl.when(s < LAST)
    def _():
        arrived(key_next.at[0], k_sem, (1,))
        arrived(key_next.at[1], k_sem, (2,))

    column(0)
    column(1)
    gather_step(1)
    term(0)
    sum_start()
    column(2)
    column(3)
    gather_step(2)
    column(4)
    column(5)
    term(1)
    term(2)
    sum_step(0)
    term(3)
    term(4)
    sum_step(1)
    term(5)
    sum_step(2)

    for n in range(6):
        arrived(got_c.at[n], c_sem, (n,))
        o = owner((GET_ODD[n], GET_EVEN[n]), odd)
        cols[pl.ds(pl.multiple_of(ROWS * o, 8), ROWS), :] = got_c[n].astype(F32)[:ROWS]

    for c, (at, size) in enumerate(CHUNKS):
        rows = pl.ds(at, size)

        @pl.when(even)
        def _():
            arrived(part_in.at[rows], x_sem, (c,))
            total_in[rows] = (
                part[rows].astype(F32) + part_in[rows].astype(F32)
            ).astype(BF16)

        push(total_in.at[rows], total_in.at[rows], t_sem, ((c,), (c,)), mate, even)

    for i in range(WIDTH // 512):
        out_ref[:, pl.ds(512 * i, 512)] = cols[pl.ds(512 * i, 512), :].T.astype(BF16)

    for c, (at, size) in enumerate(CHUNKS):
        rows = pl.ds(at, size)
        pl.when(is_odd)(lambda: arrived(total_in.at[rows], t_sem, (c,)))
    grad_ref[...] = total_in[...].astype(F32)[:ROWS].astype(BF16)

    for when, copy in pending:
        if when is None:
            copy.wait_send()
        else:
            pl.when(when)(copy.wait_send)


def per_device(normed, key_cotangent, positions, key_weight):
    index = np.arange(HEAD) % (HEAD // 2)
    freq = jnp.asarray(np.power(500000.0, -2.0 * index / HEAD)[None], F32)
    vmem = pl.BlockSpec(memory_space=pltpu.VMEM)
    dma = pltpu.SemaphoreType.DMA
    grad, passed = pl.pallas_call(
        kernel,
        out_shape=(
            jax.ShapeDtypeStruct((ROWS, KW), BF16),
            jax.ShapeDtypeStruct((TOK, WIDTH), BF16),
        ),
        in_specs=[pl.BlockSpec(memory_space=pl.ANY)] + [vmem] * 4,
        out_specs=(vmem, vmem),
        scratch_shapes=[
            pltpu.VMEM((TOK, WIDTH), BF16),
            pltpu.VMEM((RING * ROWS + 8, TOK), F32),
            pltpu.VMEM((6, PAD, TOK), BF16),
            pltpu.VMEM((6, PAD, TOK), BF16),
            pltpu.VMEM((2, TOK, KW), BF16),
            pltpu.VMEM((2, TOK, KW), BF16),
            pltpu.VMEM((PAD, KW), BF16),
            pltpu.VMEM((6, PAD, KW), BF16),
            pltpu.VMEM((6, PAD, KW), BF16),
            pltpu.VMEM((2, 3, PAD, KW), BF16),
            pltpu.VMEM((RING * ROWS, TOK), F32),
            pltpu.VMEM((6, PAD, TOK), BF16),
            pltpu.VMEM((6, PAD, TOK), BF16),
            pltpu.VMEM((PAD, KW), BF16),
            pltpu.VMEM((PAD, KW), BF16),
            pltpu.VMEM((PAD, KW), BF16),
            dma,
            dma((2, NC)),
            dma((2, 3)),
            dma((2, 6)),
            dma((2, 2, 3, NC)),
            dma((2, 2, 3, NC)),
            dma((2, 6)),
            dma((2, NC)),
            dma((2, NC)),
        ],
        compiler_params=pltpu.CompilerParams(
            collective_id=0, has_side_effects=True, vmem_limit_bytes=52 << 20
        ),
        cost_estimate=pl.CostEstimate(
            flops=4 * TOK * KW * WIDTH, bytes_accessed=6 << 20, transcendentals=2 * TOK * HEAD
        ),
    )(
        normed.reshape(TOK, WIDTH),
        key_cotangent.reshape(TOK, KW),
        positions,
        freq,
        key_weight.reshape(ROWS, KW),
    )
    return grad[None], passed.reshape(normed.shape)


def solution(mesh):
    in_specs = (
        P("section", None, ("shard", "replica"), None),
        P("section", None, ("shard", "replica"), None),
        P(None, ("shard", "replica")),
        P("section", "shard", None),
    )
    out_specs = (P("section", "shard", None), P("section", None, ("shard", "replica"), None))
    return jax.shard_map(
        per_device, mesh=mesh, in_specs=in_specs, out_specs=out_specs, check_vma=False
    )
```

```python
import functools

import jax
import jax.numpy as jnp
import numpy as np
from jax import lax
from jax.experimental import pallas as pl
from jax.experimental.pallas import tpu as pltpu
from jax.sharding import PartitionSpec as P

HEAD = 128
RING = 12
ROWS = 344
PAD = 352
KW = 512
TOK = 256
WIDTH = 4096
LAST = 15
FAR = 8
CHUNKS = ((0, 96), (96, 96), (192, 80), (272, 80))
NC = len(CHUNKS)
MESH = pl.DeviceIdType.MESH
SUM_EVEN, SUM_ODD = (6, 4, -4, 2, -2, 0), (5, -5, 3, -3, 1, -1)
GET_EVEN, GET_ODD = (0, -2, 2, -4, 4, -6), (-1, 1, -3, 3, -5, 5)
F32, BF16 = jnp.float32, jnp.bfloat16


def kernel(
    normed_hbm, cot_hbm, pos_hbm, w_hbm,
    grad_ref, out_ref,
    normed, cot_ref, pos_ref, w_ref, flat, send_n, got_n, key, key_next, wsrc, weights, terms, sums,
    cols, send_c, got_c, part, part_in, total_in,
    local_sem, w_sem, k_sem, n_sem, g_sem, r_sem, c_sem, p_sem, x_sem, t_sem,
):
    s, z, r = (lax.axis_index(a) for a in ("section", "shard", "replica"))
    inner = jnp.logical_or(r == 1, r == 2)
    outer = jnp.logical_not(inner)
    odd = lax.rem(z + inner.astype(jnp.int32), 2)
    even = odd == 0
    is_odd = odd == 1
    sign = 1 - 2 * lax.rem(s, 2)
    mate_at = r + 1 - 2 * lax.rem(r, 2)
    mate = (s, z, mate_at)
    across = (s, z, 3 - r)
    ahead = (s, lax.rem(z + sign + RING, RING), r)
    behind = (s, lax.rem(z - sign + RING, RING), r)
    lower, upper = jnp.maximum(s - 1, 0), jnp.minimum(s + 1, LAST)
    far_out, far_in = s == FAR, s == FAR - 1
    near_out = jnp.logical_and(s > 0, s != FAR)
    before = (lower, z, r)
    after = (upper, z, r)
    far_before = (lower, z, mate_at)
    far_after = (upper, z, mate_at)
    side = lax.rem(z, 2)
    far_to = (lower, z, jnp.where(r == 3, side, 3 - side))
    far_from = (upper, z, jnp.where(r < 2, 3, 0))
    far_w_out = jnp.logical_and(far_out, outer)
    far_w_in = jnp.logical_and(far_in, even)
    to = (ahead, behind)

    def owner(pair, which):
        step = jnp.where(which == 0, pair[0], pair[1])
        return lax.rem(z + sign * step + 2 * RING, RING)

    pending, chunked = [], []

    def push(src, dst, sems, index, device, when=None):
        copy = pltpu.make_async_remote_copy(
            src, dst, sems.at[(0,) + index[0]], sems.at[(1,) + index[1]],
            device_id=device, device_id_type=MESH,
        )
        if when is None:
            copy.start()
        else:
            pl.when(when)(copy.start)
        pending.append((when, copy))

    def rows(c):
        return pl.ds(*CHUNKS[c])

    def chunks(body):
        for c in range(NC):
            body(c)

    def line(src, dst, sems, index, device, when=None):
        def copy(c):
            return pltpu.make_async_remote_copy(
                src.at[rows(c)], dst.at[rows(c)],
                sems.at[(0,) + index[0] + (c,)], sems.at[(1,) + index[1] + (c,)],
                device_id=device, device_id_type=MESH,
            )

        def run(act):
            if when is None:
                act()
            else:
                pl.when(when)(act)

        chunked.append(lambda c: run(lambda: copy(c).wait_send()))
        return lambda c: run(lambda: copy(c).start())

    def arrived(dst, sems, index):
        pltpu.make_async_remote_copy(
            dst, dst, sems.at[(0,) + index], sems.at[(1,) + index],
            device_id=mate, device_id_type=MESH,
        ).wait_recv()

    fetch = [
        pltpu.make_async_copy(src, dst, local_sem.at[i])
        for i, (src, dst) in enumerate(
            ((w_hbm, w_ref), (normed_hbm, normed), (cot_hbm, cot_ref), (pos_hbm, pos_ref))
        )
    ]
    for copy in fetch:
        copy.start()
    barrier = pltpu.get_barrier_semaphore()
    count = jnp.int32(3)
    for when, device in (
        (None, mate), (None, ahead), (None, behind), (inner, across),
        (s > 0, before), (s < LAST, after), (far_out, far_before), (far_in, far_after),
        (far_w_out, far_to), (far_w_in, far_from),
    ):
        def greet():
            pl.semaphore_signal(barrier, inc=1, device_id=device, device_id_type=MESH)

        if when is None:
            greet()
        else:
            pl.when(when)(greet)
            count = count + when.astype(jnp.int32)

    fetch[0].wait()
    wsrc[...] = jnp.concatenate(
        [w_ref[...].astype(F32), jnp.zeros((PAD - ROWS, KW), F32)], axis=0
    ).astype(BF16)

    fetch[1].wait()
    for i in range(WIDTH // 512):
        flat[pl.ds(512 * i, 512), :] = normed[:, pl.ds(512 * i, 512)].astype(F32).T
    flat[pl.ds(WIDTH, 40), :] = jnp.zeros((40, TOK), F32)

    def block(o):
        return flat[pl.ds(pl.multiple_of(ROWS * o, 8), PAD), :].astype(BF16)

    pl.semaphore_wait(barrier, count)

    mine = lax.div(z, 2)
    w_near = line(wsrc, weights.at[mine], w_sem, ((), ()), before,
                  jnp.logical_and(near_out, even))
    w_far = line(wsrc, weights.at[mine], w_sem, ((), ()), far_to, far_w_out)

    @chunks
    def _(c):
        w_near(c)
        w_far(c)

    def give(n):
        send_n[n] = block(owner((SUM_ODD[n], SUM_EVEN[n]), odd))
        push(send_n.at[n], got_n.at[n], n_sem, ((n,), (n,)), mate)

    def rotate():
        fetch[2].wait()
        fetch[3].wait()
        tokens = TOK // 2
        half = lax.broadcasted_iota(jnp.int32, (tokens, HEAD), 1) < HEAD // 2
        place = [
            jnp.broadcast_to(pos_ref[m : m + 1, :].astype(F32), (HEAD, HEAD)).T for m in range(2)
        ]
        index = lax.rem(lax.broadcasted_iota(jnp.int32, (1, HEAD), 1), HEAD // 2)
        freq = jnp.exp(index.astype(F32) * np.float32(-2.0 * np.log(500000.0) / HEAD))
        angle = jnp.where(half, place[0], place[1]) * freq
        here = (jnp.cos(angle), jnp.sin(angle))
        other = [pltpu.roll(v, HEAD // 2, 1) for v in here]
        for m in range(2):
            first, second = (here, other) if m == 0 else (other, here)
            cosine, sine = (jnp.where(half, a, b) for a, b in zip(first, second))
            sine = jnp.where(half, sine, -sine)
            span = pl.ds(m * tokens, tokens)
            for h in range(KW // HEAD):
                lanes = pl.ds(h * HEAD, HEAD)
                g = cot_ref[span, lanes].astype(F32)
                key[0, span, lanes] = (
                    g * cosine + pltpu.roll(g, HEAD // 2, 1) * sine
                ).astype(BF16)

        push(key.at[0], key.at[1], k_sem, ((0,), (0,)), mate)
        push(key.at[0], key_next.at[0], k_sem, ((1,), (1,)), before, s > 0)
        push(key.at[0], key_next.at[1], k_sem, ((2,), (2,)), far_before, far_out)

        @pl.when(s == LAST)
        def _():
            key_next[...] = jnp.zeros_like(key_next)

            @pl.when(even)
            def _():
                weights[mine] = wsrc[...]

    def own_weights():
        go = [
            line(weights.at[mine], weights.at[mine], g_sem, ((d, 0), (d, 0)), to[d], even)
            for d in range(2)
        ]

        @chunks
        def _(c):
            @pl.when(jnp.logical_and(s < LAST, even))
            def _():
                arrived(weights.at[mine, rows(c)], w_sem, (c,))

            for d in range(2):
                go[d](c)

    def key_forward():
        arrived(key.at[1], k_sem, (0,))
        push(key.at[1], key_next.at[1], k_sem, ((2,), (2,)), before, near_out)

    def term(n):
        arrived(got_n.at[n], n_sem, (n,))
        own = block(owner((SUM_EVEN[n], SUM_ODD[n]), odd))
        terms[n] = (
            jnp.dot(own, key[0], preferred_element_type=F32)
            + jnp.dot(got_n[n], key[1], preferred_element_type=F32)
        ).astype(BF16)

    def gather_step(j):
        spots, go = [], []
        for d in range(2):
            away = 2 * j + 2 - odd
            from_ = lax.rem(z + (2 * d - 1) * sign * away + 2 * RING, RING)
            spot = weights.at[lax.div(from_, 2)]
            slot = j + 1 - odd if j < 2 else 2
            spots.append(spot)
            if (j, d) != (2, 1):
                go.append(line(spot, spot, g_sem, ((d, slot), (d, slot)), to[d],
                               None if j < 2 else is_odd))

        @chunks
        def _(c):
            for d in range(2):
                def get():
                    arrived(spots[d].at[rows(c)], g_sem, (d, j, c))

                if (j, d) == (2, 1):
                    pl.when(is_odd)(get)
                else:
                    get()
                    go[d](c)

    def column(n):
        o = owner((GET_EVEN[n], GET_ODD[n]), odd)
        both = lax.dot_general(
            weights[lax.div(o, 2)], key_next[...].reshape(2 * TOK, KW),
            (((1,), (1,)), ((), ())), preferred_element_type=F32,
        )
        cols[pl.ds(pl.multiple_of(ROWS * o, 8), ROWS), :] = both[:ROWS, :TOK]
        send_c[n] = both[:, TOK:].astype(BF16)
        push(send_c.at[n], got_c.at[n], c_sem, ((n,), (n,)), mate)

    def sum_start():
        go = [
            line(terms.at[d], sums.at[d, 0], r_sem, ((d, 0), (d, 0)), to[d], when)
            for d, when in enumerate((even, is_odd))
        ]

        @chunks
        def _(c):
            for d in range(2):
                go[d](c)

    def sum_step(j):
        go, number = [], []
        for d in range(2):
            spot = sums.at[d, j]
            slot = j + 1 - odd if j < 2 else 2
            when = even if (d, j) == (1, 0) else None if j < 2 else is_odd
            go.append(line(spot, sums.at[d, slot], r_sem, ((d, slot), (d, slot)), to[d], when))
            number.append(2 * j + d + 1 - odd)
        if j == 2:
            pair = line(part, part, p_sem, ((), ()), mate, jnp.logical_and(outer, even))
            other = line(part, part_in, x_sem, ((), ()), across, jnp.logical_and(inner, even))

        @chunks
        def _(c):
            here = rows(c)
            for d in range(2):
                def add():
                    arrived(sums.at[d, j, here], r_sem, (d, j, c))
                    sums[d, j, here] = (
                        sums[d, j, here].astype(F32) + terms[number[d], here].astype(F32)
                    ).astype(BF16)

                if (d, j) == (1, 0):
                    pl.when(even)(add)
                elif j < 2:
                    add()
                else:
                    pl.when(is_odd)(add)
                go[d](c)
            if j == 2:

                @pl.when(even)
                def _():
                    for d in range(2):
                        arrived(sums.at[d, 2, here], r_sem, (d, 2, c))
                    part[here] = (
                        terms[5, here].astype(F32)
                        + sums[0, 2, here].astype(F32)
                        + sums[1, 2, here].astype(F32)
                    ).astype(BF16)

                pair(c)
                other(c)

    def keys_ready():
        @pl.when(s < LAST)
        def _():
            for m in range(2):
                arrived(key_next.at[m], k_sem, (1 + m,))

    def relay_step():
        relay = jnp.logical_and(inner, is_odd)
        go = line(part, part_in, x_sem, ((), ()), across, relay)

        @chunks
        def _(c):
            pl.when(relay)(lambda: arrived(part.at[rows(c)], p_sem, (c,)))
            go(c)

    def total_step():
        go = line(total_in, total_in, t_sem, ((), ()), mate, inner)

        @chunks
        def _(c):
            here = rows(c)

            @pl.when(inner)
            def _():
                arrived(part_in.at[here], x_sem, (c,))
                total_in[here] = (
                    part[here].astype(F32) + part_in[here].astype(F32)
                ).astype(BF16)

            go(c)

    def take(n):
        arrived(got_c.at[n], c_sem, (n,))
        o = owner((GET_ODD[n], GET_EVEN[n]), odd)
        cols[pl.ds(pl.multiple_of(ROWS * o, 8), ROWS), :] = got_c[n].astype(F32)[:ROWS]

    give(0)
    rotate()
    for n in range(1, 6):
        give(n)
    own_weights()
    gather_step(0)
    key_forward()
    gather_step(1)
    keys_ready()
    column(0)
    column(1)
    term(0)
    term(1)
    sum_start()
    column(2)
    column(3)
    gather_step(2)
    column(4)
    column(5)
    term(2)
    sum_step(0)
    term(3)
    term(4)
    sum_step(1)
    term(5)
    sum_step(2)
    relay_step()
    for n in range(4):
        take(n)
    total_step()
    take(4)
    take(5)

    for i in range(WIDTH // 512):
        out_ref[:, pl.ds(512 * i, 512)] = cols[pl.ds(512 * i, 512), :].T.astype(BF16)

    @chunks
    def _(c):
        pl.when(outer)(lambda: arrived(total_in.at[rows(c)], t_sem, (c,)))

    grad_ref[...] = total_in[...].astype(F32)[:ROWS].astype(BF16)

    for when, copy in pending:
        if when is None:
            copy.wait_send()
        else:
            pl.when(when)(copy.wait_send)

    @chunks
    def _(c):
        for finish in chunked:
            finish(c)


def per_device(normed, key_cotangent, positions, key_weight):
    vmem = pl.BlockSpec(memory_space=pltpu.VMEM)
    dma = pltpu.SemaphoreType.DMA
    grad, passed = pl.pallas_call(
        kernel,
        out_shape=(
            pltpu.VMEM((ROWS, KW), BF16),
            pltpu.VMEM((TOK, WIDTH), BF16),
        ),
        in_specs=[pl.BlockSpec(memory_space=pltpu.HBM)] * 4,
        out_specs=(vmem, vmem),
        scratch_shapes=[
            pltpu.VMEM((TOK, WIDTH), BF16),
            pltpu.VMEM((TOK, KW), BF16),
            pltpu.VMEM((2, TOK // 2), jnp.int32),
            pltpu.VMEM((ROWS, KW), BF16),
            pltpu.VMEM((RING * ROWS + 8, TOK), F32),
            pltpu.VMEM((6, PAD, TOK), BF16),
            pltpu.VMEM((6, PAD, TOK), BF16),
            pltpu.VMEM((2, TOK, KW), BF16),
            pltpu.VMEM((2, TOK, KW), BF16),
            pltpu.VMEM((PAD, KW), BF16),
            pltpu.VMEM((6, PAD, KW), BF16),
            pltpu.VMEM((6, PAD, KW), BF16),
            pltpu.VMEM((2, 3, PAD, KW), BF16),
            pltpu.VMEM((RING * ROWS, TOK), F32),
            pltpu.VMEM((6, PAD, TOK), BF16),
            pltpu.VMEM((6, PAD, TOK), BF16),
            pltpu.VMEM((PAD, KW), BF16),
            pltpu.VMEM((PAD, KW), BF16),
            pltpu.VMEM((PAD, KW), BF16),
            dma((4,)),
            dma((2, NC)),
            dma((2, 3)),
            dma((2, 6)),
            dma((2, 2, 3, NC)),
            dma((2, 2, 3, NC)),
            dma((2, 6)),
            dma((2, NC)),
            dma((2, NC)),
            dma((2, NC)),
        ],
        compiler_params=pltpu.CompilerParams(
            collective_id=0, has_side_effects=True, vmem_limit_bytes=52 << 20
        ),
        cost_estimate=pl.CostEstimate(
            flops=4 * TOK * KW * WIDTH, bytes_accessed=6 << 20, transcendentals=2 * TOK * HEAD
        ),
    )(
        normed.reshape(TOK, WIDTH),
        key_cotangent.reshape(TOK, KW),
        positions,
        key_weight.reshape(ROWS, KW),
    )
    return grad[None], passed.reshape(normed.shape)


def solution(mesh):
    in_specs = (
        P("section", None, ("shard", "replica"), None),
        P("section", None, ("shard", "replica"), None),
        P(None, ("shard", "replica")),
        P("section", "shard", None),
    )
    out_specs = (P("section", "shard", None), P("section", None, ("shard", "replica"), None))
    return jax.shard_map(
        per_device, mesh=mesh, in_specs=in_specs, out_specs=out_specs, check_vma=False
    )
```

```python
import functools

import jax
import jax.numpy as jnp
import numpy as np
from jax import lax
from jax.experimental import pallas as pl
from jax.experimental.pallas import tpu as pltpu
from jax.sharding import PartitionSpec as P

HEAD = 128
RING = 12
ROWS = 344
PAD = 352
KW = 512
TOK = 256
WIDTH = 4096
LAST = 15
FAR = 8
CHUNKS = ((0, 64), (64, 64), (128, 64), (192, 64), (256, 48), (304, 48))
NC = len(CHUNKS)
MESH = pl.DeviceIdType.MESH
SUM_EVEN, SUM_ODD = (6, 4, -4, 2, -2, 0), (5, -5, 3, -3, 1, -1)
GET_EVEN, GET_ODD = (0, -2, 2, -4, 4, -6), (-1, 1, -3, 3, -5, 5)
F32, BF16 = jnp.float32, jnp.bfloat16


def kernel(
    normed_hbm, cot_hbm, pos_hbm, w_hbm,
    grad_ref, out_ref,
    normed, cot_ref, pos_ref, w_ref, flat, send_n, got_n, key, key_next, wsrc, weights, terms, sums,
    cols, send_c, got_c, part, part_in, total_in,
    local_sem, w_sem, k_sem, n_sem, g_sem, r_sem, c_sem, x_sem, t_sem,
):
    s, z, r = (lax.axis_index(a) for a in ("section", "shard", "replica"))
    inner = jnp.logical_or(r == 1, r == 2)
    outer = jnp.logical_not(inner)
    odd = lax.rem(z + inner.astype(jnp.int32), 2)
    even = odd == 0
    is_odd = odd == 1
    sign = 1 - 2 * lax.rem(s, 2)
    mate_at = r + 1 - 2 * lax.rem(r, 2)
    mate = (s, z, mate_at)
    across = (s, z, 3 - r)
    ahead = (s, lax.rem(z + sign + RING, RING), r)
    behind = (s, lax.rem(z - sign + RING, RING), r)
    lower, upper = jnp.maximum(s - 1, 0), jnp.minimum(s + 1, LAST)
    far_out, far_in = s == FAR, s == FAR - 1
    near_out = jnp.logical_and(s > 0, s != FAR)
    before = (lower, z, r)
    after = (upper, z, r)
    far_before = (lower, z, mate_at)
    far_after = (upper, z, mate_at)
    side = lax.rem(z, 2)
    far_to = (lower, z, jnp.where(r == 3, side, 3 - side))
    far_from = (upper, z, jnp.where(r < 2, 3, 0))
    far_w_out = jnp.logical_and(far_out, outer)
    far_w_in = jnp.logical_and(far_in, even)
    to = (ahead, behind)

    def owner(pair, which):
        step = jnp.where(which == 0, pair[0], pair[1])
        return lax.rem(z + sign * step + 2 * RING, RING)

    pending, chunked = [], []

    def push(src, dst, sems, index, device, when=None):
        copy = pltpu.make_async_remote_copy(
            src, dst, sems.at[(0,) + index[0]], sems.at[(1,) + index[1]],
            device_id=device, device_id_type=MESH,
        )
        if when is None:
            copy.start()
        else:
            pl.when(when)(copy.start)
        pending.append((when, copy))

    def rows(c):
        return pl.ds(*CHUNKS[c])

    def chunks(body):
        for c in range(NC):
            body(c)

    def line(src, dst, sems, index, device, when=None):
        def copy(c):
            return pltpu.make_async_remote_copy(
                src.at[rows(c)], dst.at[rows(c)],
                sems.at[(0,) + index[0] + (c,)], sems.at[(1,) + index[1] + (c,)],
                device_id=device, device_id_type=MESH,
            )

        def run(act):
            if when is None:
                act()
            else:
                pl.when(when)(act)

        chunked.append(lambda c: run(lambda: copy(c).wait_send()))
        return lambda c: run(lambda: copy(c).start())

    def arrived(dst, sems, index):
        pltpu.make_async_remote_copy(
            dst, dst, sems.at[(0,) + index], sems.at[(1,) + index],
            device_id=mate, device_id_type=MESH,
        ).wait_recv()

    fetch = [
        pltpu.make_async_copy(src, dst, local_sem.at[i])
        for i, (src, dst) in enumerate(
            ((w_hbm, w_ref), (normed_hbm, normed), (cot_hbm, cot_ref), (pos_hbm, pos_ref))
        )
    ]
    for copy in fetch:
        copy.start()
    barrier = pltpu.get_barrier_semaphore()
    count = jnp.int32(4)
    for when, device in (
        (None, mate), (None, across), (None, ahead), (None, behind),
        (s > 0, before), (s < LAST, after), (far_out, far_before), (far_in, far_after),
        (far_w_out, far_to), (far_w_in, far_from),
    ):
        def greet():
            pl.semaphore_signal(barrier, inc=1, device_id=device, device_id_type=MESH)

        if when is None:
            greet()
        else:
            pl.when(when)(greet)
            count = count + when.astype(jnp.int32)

    fetch[0].wait()
    wsrc[...] = jnp.concatenate(
        [w_ref[...].astype(F32), jnp.zeros((PAD - ROWS, KW), F32)], axis=0
    ).astype(BF16)

    pl.semaphore_wait(barrier, count)

    mine = lax.div(z, 2)
    w_near = line(wsrc, weights.at[mine], w_sem, ((), ()), before,
                  jnp.logical_and(near_out, even))
    w_far = line(wsrc, weights.at[mine], w_sem, ((), ()), far_to, far_w_out)

    @chunks
    def _(c):
        w_near(c)
        w_far(c)

    fetch[1].wait()
    for i in range(WIDTH // 512):
        flat[pl.ds(512 * i, 512), :] = normed[:, pl.ds(512 * i, 512)].astype(F32).T
    flat[pl.ds(WIDTH, 40), :] = jnp.zeros((40, TOK), F32)

    def block(o):
        return flat[pl.ds(pl.multiple_of(ROWS * o, 8), PAD), :].astype(BF16)

    def give(n):
        send_n[n] = block(owner((SUM_ODD[n], SUM_EVEN[n]), odd))
        push(send_n.at[n], got_n.at[n], n_sem, ((n,), (n,)), mate)

    def rotate():
        fetch[2].wait()
        fetch[3].wait()
        tokens = TOK // 2
        half = lax.broadcasted_iota(jnp.int32, (tokens, HEAD), 1) < HEAD // 2
        place = [
            jnp.broadcast_to(pos_ref[m : m + 1, :].astype(F32), (HEAD, HEAD)).T for m in range(2)
        ]
        index = lax.rem(lax.broadcasted_iota(jnp.int32, (1, HEAD), 1), HEAD // 2)
        freq = jnp.exp(index.astype(F32) * np.float32(-2.0 * np.log(500000.0) / HEAD))
        angle = jnp.where(half, place[0], place[1]) * freq
        here = (jnp.cos(angle), jnp.sin(angle))
        other = [pltpu.roll(v, HEAD // 2, 1) for v in here]
        for m in range(2):
            first, second = (here, other) if m == 0 else (other, here)
            cosine, sine = (jnp.where(half, a, b) for a, b in zip(first, second))
            sine = jnp.where(half, sine, -sine)
            span = pl.ds(m * tokens, tokens)
            for h in range(KW // HEAD):
                lanes = pl.ds(h * HEAD, HEAD)
                g = cot_ref[span, lanes].astype(F32)
                key[0, span, lanes] = (
                    g * cosine + pltpu.roll(g, HEAD // 2, 1) * sine
                ).astype(BF16)

        push(key.at[0], key.at[1], k_sem, ((0,), (0,)), mate)
        push(key.at[0], key_next.at[0], k_sem, ((1,), (1,)), before, s > 0)
        push(key.at[0], key_next.at[1], k_sem, ((2,), (2,)), far_before, far_out)

        @pl.when(s == LAST)
        def _():
            key_next[...] = jnp.zeros_like(key_next)

            @pl.when(even)
            def _():
                weights[mine] = wsrc[...]

    def own_weights():
        go = [
            line(weights.at[mine], weights.at[mine], g_sem, ((d, 0), (d, 0)), to[d], even)
            for d in range(2)
        ]

        @chunks
        def _(c):
            @pl.when(jnp.logical_and(s < LAST, even))
            def _():
                arrived(weights.at[mine, rows(c)], w_sem, (c,))

            for d in range(2):
                go[d](c)

    def key_forward():
        arrived(key.at[1], k_sem, (0,))
        push(key.at[1], key_next.at[1], k_sem, ((2,), (2,)), before, near_out)

    def term(n):
        arrived(got_n.at[n], n_sem, (n,))
        own = block(owner((SUM_EVEN[n], SUM_ODD[n]), odd))
        terms[n] = (
            jnp.dot(own, key[0], preferred_element_type=F32)
            + jnp.dot(got_n[n], key[1], preferred_element_type=F32)
        ).astype(BF16)

    def gather_step(j):
        spots, go = [], []
        for d in range(2):
            away = 2 * j + 2 - odd
            from_ = lax.rem(z + (2 * d - 1) * sign * away + 2 * RING, RING)
            spot = weights.at[lax.div(from_, 2)]
            slot = j + 1 - odd if j < 2 else 2
            spots.append(spot)
            if (j, d) != (2, 1):
                go.append(line(spot, spot, g_sem, ((d, slot), (d, slot)), to[d],
                               None if j < 2 else is_odd))

        @chunks
        def _(c):
            for d in range(2):
                def get():
                    arrived(spots[d].at[rows(c)], g_sem, (d, j, c))

                if (j, d) == (2, 1):
                    pl.when(is_odd)(get)
                else:
                    get()
                    go[d](c)

    def column(n):
        o = owner((GET_EVEN[n], GET_ODD[n]), odd)
        both = lax.dot_general(
            weights[lax.div(o, 2)], key_next[...].reshape(2 * TOK, KW),
            (((1,), (1,)), ((), ())), preferred_element_type=F32,
        )
        cols[pl.ds(pl.multiple_of(ROWS * o, 8), ROWS), :] = both[:ROWS, :TOK]
        send_c[n] = both[:, TOK:].astype(BF16)
        push(send_c.at[n], got_c.at[n], c_sem, ((n,), (n,)), mate)

    def sum_start():
        go = [
            line(terms.at[d], sums.at[d, 0], r_sem, ((d, 0), (d, 0)), to[d], when)
            for d, when in enumerate((even, is_odd))
        ]

        @chunks
        def _(c):
            for d in range(2):
                go[d](c)

    def sum_step(j):
        go, number = [], []
        for d in range(2):
            spot = sums.at[d, j]
            slot = j + 1 - odd if j < 2 else 2
            when = even if (d, j) == (1, 0) else None if j < 2 else is_odd
            go.append(line(spot, sums.at[d, slot], r_sem, ((d, slot), (d, slot)), to[d], when))
            number.append(2 * j + d + 1 - odd)
        if j == 2:
            other = line(part, part_in, x_sem, ((), ()), across, even)

        @chunks
        def _(c):
            here = rows(c)
            for d in range(2):
                def add():
                    arrived(sums.at[d, j, here], r_sem, (d, j, c))
                    sums[d, j, here] = (
                        sums[d, j, here].astype(F32) + terms[number[d], here].astype(F32)
                    ).astype(BF16)

                if (d, j) == (1, 0):
                    pl.when(even)(add)
                elif j < 2:
                    add()
                else:
                    pl.when(is_odd)(add)
                go[d](c)
            if j == 2:

                @pl.when(even)
                def _():
                    for d in range(2):
                        arrived(sums.at[d, 2, here], r_sem, (d, 2, c))
                    part[here] = (
                        terms[5, here].astype(F32)
                        + sums[0, 2, here].astype(F32)
                        + sums[1, 2, here].astype(F32)
                    ).astype(BF16)

                other(c)

    def keys_ready():
        @pl.when(s < LAST)
        def _():
            for m in range(2):
                arrived(key_next.at[m], k_sem, (1 + m,))

    def total_step():
        go = line(total_in, total_in, t_sem, ((), ()), mate, even)

        @chunks
        def _(c):
            here = rows(c)

            @pl.when(even)
            def _():
                arrived(part_in.at[here], x_sem, (c,))
                total_in[here] = (
                    part[here].astype(F32) + part_in[here].astype(F32)
                ).astype(BF16)

            go(c)

    def take(n):
        arrived(got_c.at[n], c_sem, (n,))
        o = owner((GET_ODD[n], GET_EVEN[n]), odd)
        cols[pl.ds(pl.multiple_of(ROWS * o, 8), ROWS), :] = got_c[n].astype(F32)[:ROWS]

    give(0)
    rotate()
    for n in range(1, 6):
        give(n)
    own_weights()
    gather_step(0)
    key_forward()
    gather_step(1)
    keys_ready()
    column(0)
    column(1)
    term(0)
    term(1)
    sum_start()
    column(2)
    column(3)
    gather_step(2)
    column(4)
    column(5)
    term(2)
    sum_step(0)
    term(3)
    term(4)
    sum_step(1)
    term(5)
    sum_step(2)
    total_step()
    for n in range(6):
        take(n)

    for i in range(WIDTH // 512):
        out_ref[:, pl.ds(512 * i, 512)] = cols[pl.ds(512 * i, 512), :].T.astype(BF16)

    @chunks
    def _(c):
        pl.when(is_odd)(lambda: arrived(total_in.at[rows(c)], t_sem, (c,)))

    grad_ref[...] = total_in[...].astype(F32)[:ROWS].astype(BF16)

    for when, copy in pending:
        if when is None:
            copy.wait_send()
        else:
            pl.when(when)(copy.wait_send)

    @chunks
    def _(c):
        for finish in chunked:
            finish(c)


def per_device(normed, key_cotangent, positions, key_weight):
    vmem = pl.BlockSpec(memory_space=pltpu.VMEM)
    dma = pltpu.SemaphoreType.DMA
    grad, passed = pl.pallas_call(
        kernel,
        out_shape=(
            pltpu.VMEM((ROWS, KW), BF16),
            pltpu.VMEM((TOK, WIDTH), BF16),
        ),
        in_specs=[pl.BlockSpec(memory_space=pltpu.HBM)] * 4,
        out_specs=(vmem, vmem),
        scratch_shapes=[
            pltpu.VMEM((TOK, WIDTH), BF16),
            pltpu.VMEM((TOK, KW), BF16),
            pltpu.VMEM((2, TOK // 2), jnp.int32),
            pltpu.VMEM((ROWS, KW), BF16),
            pltpu.VMEM((RING * ROWS + 8, TOK), F32),
            pltpu.VMEM((6, PAD, TOK), BF16),
            pltpu.VMEM((6, PAD, TOK), BF16),
            pltpu.VMEM((2, TOK, KW), BF16),
            pltpu.VMEM((2, TOK, KW), BF16),
            pltpu.VMEM((PAD, KW), BF16),
            pltpu.VMEM((6, PAD, KW), BF16),
            pltpu.VMEM((6, PAD, KW), BF16),
            pltpu.VMEM((2, 3, PAD, KW), BF16),
            pltpu.VMEM((RING * ROWS, TOK), F32),
            pltpu.VMEM((6, PAD, TOK), BF16),
            pltpu.VMEM((6, PAD, TOK), BF16),
            pltpu.VMEM((PAD, KW), BF16),
            pltpu.VMEM((PAD, KW), BF16),
            pltpu.VMEM((PAD, KW), BF16),
            dma((4,)),
            dma((2, NC)),
            dma((2, 3)),
            dma((2, 6)),
            dma((2, 2, 3, NC)),
            dma((2, 2, 3, NC)),
            dma((2, 6)),
            dma((2, NC)),
            dma((2, NC)),
        ],
        compiler_params=pltpu.CompilerParams(
            collective_id=0, has_side_effects=True, vmem_limit_bytes=52 << 20
        ),
        cost_estimate=pl.CostEstimate(
            flops=4 * TOK * KW * WIDTH, bytes_accessed=6 << 20, transcendentals=2 * TOK * HEAD
        ),
    )(
        normed.reshape(TOK, WIDTH),
        key_cotangent.reshape(TOK, KW),
        positions,
        key_weight.reshape(ROWS, KW),
    )
    return grad[None], passed.reshape(normed.shape)


def solution(mesh):
    in_specs = (
        P("section", None, ("shard", "replica"), None),
        P("section", None, ("shard", "replica"), None),
        P(None, ("shard", "replica")),
        P("section", "shard", None),
    )
    out_specs = (P("section", "shard", None), P("section", None, ("shard", "replica"), None))
    return jax.shard_map(
        per_device, mesh=mesh, in_specs=in_specs, out_specs=out_specs, check_vma=False
    )
```

```python
import functools

import jax
import jax.numpy as jnp
import numpy as np
from jax import lax
from jax.experimental import pallas as pl
from jax.experimental.pallas import tpu as pltpu
from jax.sharding import PartitionSpec as P

HEAD = 128
RING = 12
ROWS = 344
PAD = 352
KW = 512
TOK = 256
WIDTH = 4096
LAST = 15
FAR = 8
CHUNKS = ((0, 96), (96, 96), (192, 80), (272, 80))
NC = len(CHUNKS)
MESH = pl.DeviceIdType.MESH
SUM_EVEN, SUM_ODD = (6, 4, -4, 2, -2, 0), (5, -5, 3, -3, 1, -1)
GET_EVEN, GET_ODD = (0, -2, 2, -4, 4, -6), (-1, 1, -3, 3, -5, 5)
F32, BF16 = jnp.float32, jnp.bfloat16


def kernel(
    normed_hbm, cot_hbm, pos_hbm, w_hbm,
    grad_ref, out_ref,
    normed, cot_ref, pos_ref, w_ref, flat, send_n, got_n, key, key_next, wsrc, weights, terms, sums,
    cols, send_c, got_c, part, part_in, total_in,
    local_sem, w_sem, k_sem, n_sem, g_sem, r_sem, c_sem, p_sem, x_sem, t_sem,
):
    s, z, r = (lax.axis_index(a) for a in ("section", "shard", "replica"))
    inner = jnp.logical_or(r == 1, r == 2)
    outer = jnp.logical_not(inner)
    odd = lax.rem(z + inner.astype(jnp.int32), 2)
    even = odd == 0
    is_odd = odd == 1
    sign = 1 - 2 * lax.rem(s, 2)
    mate_at = r + 1 - 2 * lax.rem(r, 2)
    mate = (s, z, mate_at)
    across = (s, z, 3 - r)
    ahead = (s, lax.rem(z + sign + RING, RING), r)
    behind = (s, lax.rem(z - sign + RING, RING), r)
    lower, upper = jnp.maximum(s - 1, 0), jnp.minimum(s + 1, LAST)
    far_out, far_in = s == FAR, s == FAR - 1
    near_out = jnp.logical_and(s > 0, s != FAR)
    before = (lower, z, r)
    after = (upper, z, r)
    far_before = (lower, z, mate_at)
    far_after = (upper, z, mate_at)
    side = lax.rem(z, 2)
    far_to = (lower, z, jnp.where(r == 3, side, 3 - side))
    far_from = (upper, z, jnp.where(r < 2, 3, 0))
    far_w_out = jnp.logical_and(far_out, outer)
    far_w_in = jnp.logical_and(far_in, even)
    to = (ahead, behind)

    def owner(pair, which):
        step = jnp.where(which == 0, pair[0], pair[1])
        return lax.rem(z + sign * step + 2 * RING, RING)

    pending, chunked = [], []

    def push(src, dst, sems, index, device, when=None):
        copy = pltpu.make_async_remote_copy(
            src, dst, sems.at[(0,) + index[0]], sems.at[(1,) + index[1]],
            device_id=device, device_id_type=MESH,
        )
        if when is None:
            copy.start()
        else:
            pl.when(when)(copy.start)
        pending.append((when, copy))

    def rows(c):
        return pl.ds(*CHUNKS[c])

    def chunks(body):
        for c in range(NC):
            body(c)

    def line(src, dst, sems, index, device, when=None):
        def copy(c):
            return pltpu.make_async_remote_copy(
                src.at[rows(c)], dst.at[rows(c)],
                sems.at[(0,) + index[0] + (c,)], sems.at[(1,) + index[1] + (c,)],
                device_id=device, device_id_type=MESH,
            )

        def run(act):
            if when is None:
                act()
            else:
                pl.when(when)(act)

        chunked.append(lambda c: run(lambda: copy(c).wait_send()))
        return lambda c: run(lambda: copy(c).start())

    def arrived(dst, sems, index):
        pltpu.make_async_remote_copy(
            dst, dst, sems.at[(0,) + index], sems.at[(1,) + index],
            device_id=mate, device_id_type=MESH,
        ).wait_recv()

    fetch = [
        pltpu.make_async_copy(src, dst, local_sem.at[i])
        for i, (src, dst) in enumerate(
            ((w_hbm, w_ref), (normed_hbm, normed), (cot_hbm, cot_ref), (pos_hbm, pos_ref))
        )
    ]
    for copy in fetch:
        copy.start()
    barrier = pltpu.get_barrier_semaphore()
    count = jnp.int32(3)
    for when, device in (
        (None, mate), (None, ahead), (None, behind), (inner, across),
        (s > 0, before), (s < LAST, after), (far_out, far_before), (far_in, far_after),
        (far_w_out, far_to), (far_w_in, far_from),
    ):
        def greet():
            pl.semaphore_signal(barrier, inc=1, device_id=device, device_id_type=MESH)

        if when is None:
            greet()
        else:
            pl.when(when)(greet)
            count = count + when.astype(jnp.int32)

    fetch[0].wait()
    wsrc[...] = jnp.concatenate(
        [w_ref[...].astype(F32), jnp.zeros((PAD - ROWS, KW), F32)], axis=0
    ).astype(BF16)

    pl.semaphore_wait(barrier, count)

    mine = lax.div(z, 2)
    w_near = line(wsrc, weights.at[mine], w_sem, ((), ()), before,
                  jnp.logical_and(near_out, even))
    w_far = line(wsrc, weights.at[mine], w_sem, ((), ()), far_to, far_w_out)

    @chunks
    def _(c):
        w_near(c)
        w_far(c)

    fetch[1].wait()
    for i in range(WIDTH // 512):
        flat[pl.ds(512 * i, 512), :] = normed[:, pl.ds(512 * i, 512)].astype(F32).T
    flat[pl.ds(WIDTH, 40), :] = jnp.zeros((40, TOK), F32)

    def block(o):
        return flat[pl.ds(pl.multiple_of(ROWS * o, 8), PAD), :].astype(BF16)

    def give(n):
        send_n[n] = block(owner((SUM_ODD[n], SUM_EVEN[n]), odd))
        push(send_n.at[n], got_n.at[n], n_sem, ((n,), (n,)), mate)

    def rotate():
        fetch[2].wait()
        fetch[3].wait()
        tokens = TOK // 2
        half = lax.broadcasted_iota(jnp.int32, (tokens, HEAD), 1) < HEAD // 2
        place = [
            jnp.broadcast_to(pos_ref[m : m + 1, :].astype(F32), (HEAD, HEAD)).T for m in range(2)
        ]
        index = lax.rem(lax.broadcasted_iota(jnp.int32, (1, HEAD), 1), HEAD // 2)
        freq = jnp.exp(index.astype(F32) * np.float32(-2.0 * np.log(500000.0) / HEAD))
        angle = jnp.where(half, place[0], place[1]) * freq
        here = (jnp.cos(angle), jnp.sin(angle))
        other = [pltpu.roll(v, HEAD // 2, 1) for v in here]
        for m in range(2):
            first, second = (here, other) if m == 0 else (other, here)
            cosine, sine = (jnp.where(half, a, b) for a, b in zip(first, second))
            sine = jnp.where(half, sine, -sine)
            span = pl.ds(m * tokens, tokens)
            for h in range(KW // HEAD):
                lanes = pl.ds(h * HEAD, HEAD)
                g = cot_ref[span, lanes].astype(F32)
                key[0, span, lanes] = (
                    g * cosine + pltpu.roll(g, HEAD // 2, 1) * sine
                ).astype(BF16)

        push(key.at[0], key.at[1], k_sem, ((0,), (0,)), mate)
        push(key.at[0], key_next.at[0], k_sem, ((1,), (1,)), before, s > 0)
        push(key.at[0], key_next.at[1], k_sem, ((2,), (2,)), far_before, far_out)

        @pl.when(s == LAST)
        def _():
            key_next[...] = jnp.zeros_like(key_next)

            @pl.when(even)
            def _():
                weights[mine] = wsrc[...]

    def own_weights():
        go = [
            line(weights.at[mine], weights.at[mine], g_sem, ((d, 0), (d, 0)), to[d], even)
            for d in range(2)
        ]

        @chunks
        def _(c):
            @pl.when(jnp.logical_and(s < LAST, even))
            def _():
                arrived(weights.at[mine, rows(c)], w_sem, (c,))

            for d in range(2):
                go[d](c)

    def key_forward():
        arrived(key.at[1], k_sem, (0,))
        push(key.at[1], key_next.at[1], k_sem, ((2,), (2,)), before, near_out)

    def term(n):
        arrived(got_n.at[n], n_sem, (n,))
        own = block(owner((SUM_EVEN[n], SUM_ODD[n]), odd))
        terms[n] = (
            jnp.dot(own, key[0], preferred_element_type=F32)
            + jnp.dot(got_n[n], key[1], preferred_element_type=F32)
        ).astype(BF16)

    def gather_step(j):
        spots, go = [], []
        for d in range(2):
            away = 2 * j + 2 - odd
            from_ = lax.rem(z + (2 * d - 1) * sign * away + 2 * RING, RING)
            spot = weights.at[lax.div(from_, 2)]
            slot = j + 1 - odd if j < 2 else 2
            spots.append(spot)
            if (j, d) != (2, 1):
                go.append(line(spot, spot, g_sem, ((d, slot), (d, slot)), to[d],
                               None if j < 2 else is_odd))

        @chunks
        def _(c):
            for d in range(2):
                def get():
                    arrived(spots[d].at[rows(c)], g_sem, (d, j, c))

                if (j, d) == (2, 1):
                    pl.when(is_odd)(get)
                else:
                    get()
                    go[d](c)

    def column(n):
        o = owner((GET_EVEN[n], GET_ODD[n]), odd)
        both = lax.dot_general(
            weights[lax.div(o, 2)], key_next[...].reshape(2 * TOK, KW),
            (((1,), (1,)), ((), ())), preferred_element_type=F32,
        )
        cols[pl.ds(pl.multiple_of(ROWS * o, 8), ROWS), :] = both[:ROWS, :TOK]
        send_c[n] = both[:, TOK:].astype(BF16)
        push(send_c.at[n], got_c.at[n], c_sem, ((n,), (n,)), mate)

    def sum_start():
        go = [
            line(terms.at[d], sums.at[d, 0], r_sem, ((d, 0), (d, 0)), to[d], when)
            for d, when in enumerate((even, is_odd))
        ]

        @chunks
        def _(c):
            for d in range(2):
                go[d](c)

    def sum_step(j):
        go, number = [], []
        for d in range(2):
            spot = sums.at[d, j]
            slot = j + 1 - odd if j < 2 else 2
            when = even if (d, j) == (1, 0) else None if j < 2 else is_odd
            go.append(line(spot, sums.at[d, slot], r_sem, ((d, slot), (d, slot)), to[d], when))
            number.append(2 * j + d + 1 - odd)
        if j == 2:
            pair = line(part, part, p_sem, ((), ()), mate, jnp.logical_and(outer, even))
            other = line(part, part_in, x_sem, ((), ()), across, jnp.logical_and(inner, even))

        @chunks
        def _(c):
            here = rows(c)
            for d in range(2):
                def add():
                    arrived(sums.at[d, j, here], r_sem, (d, j, c))
                    sums[d, j, here] = (
                        sums[d, j, here].astype(F32) + terms[number[d], here].astype(F32)
                    ).astype(BF16)

                if (d, j) == (1, 0):
                    pl.when(even)(add)
                elif j < 2:
                    add()
                else:
                    pl.when(is_odd)(add)
                go[d](c)
            if j == 2:

                @pl.when(even)
                def _():
                    for d in range(2):
                        arrived(sums.at[d, 2, here], r_sem, (d, 2, c))
                    part[here] = (
                        terms[5, here].astype(F32)
                        + sums[0, 2, here].astype(F32)
                        + sums[1, 2, here].astype(F32)
                    ).astype(BF16)

                pair(c)
                other(c)

    def keys_ready():
        @pl.when(s < LAST)
        def _():
            for m in range(2):
                arrived(key_next.at[m], k_sem, (1 + m,))

    def relay_step():
        relay = jnp.logical_and(inner, is_odd)
        go = line(part, part_in, x_sem, ((), ()), across, relay)

        @chunks
        def _(c):
            pl.when(relay)(lambda: arrived(part.at[rows(c)], p_sem, (c,)))
            go(c)

    def total_step():
        go = line(total_in, total_in, t_sem, ((), ()), mate, inner)

        @chunks
        def _(c):
            here = rows(c)

            @pl.when(inner)
            def _():
                arrived(part_in.at[here], x_sem, (c,))
                total_in[here] = (
                    part[here].astype(F32) + part_in[here].astype(F32)
                ).astype(BF16)

            go(c)

    def take(n):
        arrived(got_c.at[n], c_sem, (n,))
        o = owner((GET_ODD[n], GET_EVEN[n]), odd)
        cols[pl.ds(pl.multiple_of(ROWS * o, 8), ROWS), :] = got_c[n].astype(F32)[:ROWS]

    give(0)
    rotate()
    for n in range(1, 6):
        give(n)
    own_weights()
    gather_step(0)
    key_forward()
    gather_step(1)
    term(0)
    term(1)
    sum_start()
    keys_ready()
    column(0)
    column(1)
    column(2)
    column(3)
    gather_step(2)
    column(4)
    column(5)
    term(2)
    sum_step(0)
    term(3)
    term(4)
    sum_step(1)
    term(5)
    sum_step(2)
    relay_step()
    for n in range(4):
        take(n)
    total_step()
    take(4)
    take(5)

    for i in range(WIDTH // 512):
        out_ref[:, pl.ds(512 * i, 512)] = cols[pl.ds(512 * i, 512), :].T.astype(BF16)

    @chunks
    def _(c):
        pl.when(outer)(lambda: arrived(total_in.at[rows(c)], t_sem, (c,)))

    grad_ref[...] = total_in[...].astype(F32)[:ROWS].astype(BF16)

    for when, copy in pending:
        if when is None:
            copy.wait_send()
        else:
            pl.when(when)(copy.wait_send)

    @chunks
    def _(c):
        for finish in chunked:
            finish(c)


def per_device(normed, key_cotangent, positions, key_weight):
    vmem = pl.BlockSpec(memory_space=pltpu.VMEM)
    dma = pltpu.SemaphoreType.DMA
    grad, passed = pl.pallas_call(
        kernel,
        out_shape=(
            pltpu.VMEM((ROWS, KW), BF16),
            pltpu.VMEM((TOK, WIDTH), BF16),
        ),
        in_specs=[pl.BlockSpec(memory_space=pltpu.HBM)] * 4,
        out_specs=(vmem, vmem),
        scratch_shapes=[
            pltpu.VMEM((TOK, WIDTH), BF16),
            pltpu.VMEM((TOK, KW), BF16),
            pltpu.VMEM((2, TOK // 2), jnp.int32),
            pltpu.VMEM((ROWS, KW), BF16),
            pltpu.VMEM((RING * ROWS + 8, TOK), F32),
            pltpu.VMEM((6, PAD, TOK), BF16),
            pltpu.VMEM((6, PAD, TOK), BF16),
            pltpu.VMEM((2, TOK, KW), BF16),
            pltpu.VMEM((2, TOK, KW), BF16),
            pltpu.VMEM((PAD, KW), BF16),
            pltpu.VMEM((6, PAD, KW), BF16),
            pltpu.VMEM((6, PAD, KW), BF16),
            pltpu.VMEM((2, 3, PAD, KW), BF16),
            pltpu.VMEM((RING * ROWS, TOK), F32),
            pltpu.VMEM((6, PAD, TOK), BF16),
            pltpu.VMEM((6, PAD, TOK), BF16),
            pltpu.VMEM((PAD, KW), BF16),
            pltpu.VMEM((PAD, KW), BF16),
            pltpu.VMEM((PAD, KW), BF16),
            dma((4,)),
            dma((2, NC)),
            dma((2, 3)),
            dma((2, 6)),
            dma((2, 2, 3, NC)),
            dma((2, 2, 3, NC)),
            dma((2, 6)),
            dma((2, NC)),
            dma((2, NC)),
            dma((2, NC)),
        ],
        compiler_params=pltpu.CompilerParams(
            collective_id=0, has_side_effects=True, vmem_limit_bytes=52 << 20
        ),
        cost_estimate=pl.CostEstimate(
            flops=4 * TOK * KW * WIDTH, bytes_accessed=6 << 20, transcendentals=2 * TOK * HEAD
        ),
    )(
        normed.reshape(TOK, WIDTH),
        key_cotangent.reshape(TOK, KW),
        positions,
        key_weight.reshape(ROWS, KW),
    )
    return grad[None], passed.reshape(normed.shape)


def solution(mesh):
    in_specs = (
        P("section", None, ("shard", "replica"), None),
        P("section", None, ("shard", "replica"), None),
        P(None, ("shard", "replica")),
        P("section", "shard", None),
    )
    out_specs = (P("section", "shard", None), P("section", None, ("shard", "replica"), None))
    return jax.shard_map(
        per_device, mesh=mesh, in_specs=in_specs, out_specs=out_specs, check_vma=False
    )
```
